32 devices in a mesh: row: 16 (over z, y, x), col: 2 (over core).
Axes of the slice: x: 2, y: 2, z: 4, core: 2. Of those that a mesh axis runs over, the one named last changes fastest.
Arguments:
- rhs: float32 [2, 16, 1024, 1024], P(None, 'row', None, 'col'), may hold values from -8 to 8
- panels: float32 [2, 2, 16, 1024, 1024], P(None, None, 'row', None, 'col'), may hold values from -0.1875 to 0.1875
- inverses: float32 [2, 1024, 1024], replicated, may hold values from -1 to 4, as said below
Outputs:
- result: float32 [2, 16, 1024, 1024], P(None, 'row', None, 'col')
The draws below stay inside these ranges and needn't reach their ends.
Inputs may be any that keep to these rules, and one draw needn't show every extreme that they name: Each inverses[k] is lower triangular with a positive diagonal.
All inputs are finite; a program needn't handle non-finite values.
Results may differ from the reference program's by a relative error of at most 0.000075.
Values sent between devices are 32-bit elements; how exact they have to be, the bound alone decides.
A program may use at most 128 MiB of HBM per device.

```python
import math
import jax
import jax.numpy as jnp
from jax import lax

NB = 1024
R = 1024
RBD = 2
N_ROW = 16


def draw_inverses(key, part):
    key_diag, key_off = jax.random.split(jax.random.fold_in(key, 7))
    lower_mask = (jnp.arange(NB)[:, None] > jnp.arange(NB)[None, :]).astype(jnp.float32)
    diagonal = jnp.exp(jax.random.uniform(key_diag, (2, NB), jnp.float32, -math.log(2.0), math.log(2.0)))
    off_diag = jax.random.normal(key_off, (2, NB, NB), jnp.float32) * (0.6 / math.sqrt(NB))
    return off_diag * lower_mask[None] + jnp.eye(NB, dtype=jnp.float32)[None] * diagonal[:, :, None]


def block_scale(rng, shape, shards, smallest, top_value):
    factor_of = 1.0
    for axis_at, shards_of in shards:
        draws = jax.random.uniform(jax.random.fold_in(jax.random.fold_in(rng, 6), axis_at), (shards_of,), jnp.float32, smallest / len(shards), top_value / len(shards))
        factor_of = factor_of * jnp.repeat(jnp.exp(draws), shape[axis_at] // shards_of).reshape((-1,) + (1,) * (len(shape) - 1 - axis_at))
    return factor_of


def noise(key, shape, width, reach, pieces=(), held_as=jnp.bfloat16):
    values = jax.random.normal(key, shape, jnp.float32) * width
    if len(pieces) > 0:
        values = block_scale(key, shape, pieces, -0.22, 0.18) * values
    return jnp.clip(values, min=-reach, max=reach).astype(held_as)


def setup_inputs(seed: int = 0) -> dict:
    arg_keys = jax.random.split(jax.random.key(seed), 4)
    return {
        "rhs": noise(arg_keys[0], (RBD, N_ROW, NB, R), 1.0, 8.0, ((1, 16), (3, 2)), jnp.float32),
        "panels": noise(arg_keys[1], (2, RBD, N_ROW, NB, NB), NB ** -0.5, 0.1875, ((2, 16), (4, 2)), jnp.float32),
        "inverses": draw_inverses(jax.random.fold_in(arg_keys[3], 71), 0),
    }


def reference(rhs, panels, inverses):
    highest = lax.Precision.HIGHEST
    block_ids = (jnp.arange(RBD, dtype=jnp.int32)[:, None] * N_ROW + jnp.arange(N_ROW, dtype=jnp.int32)[None, :])[:, :, None, None]
    solved0 = jnp.dot(inverses[0], rhs[0, 0], precision=highest, preferred_element_type=jnp.float32)
    update0 = jnp.einsum("sqin,nr->sqir", panels[0], solved0, precision=highest, preferred_element_type=jnp.float32)
    sectioned = jnp.where(block_ids >= 1, rhs - update0, solved0)
    solved1 = jnp.dot(inverses[1], sectioned[0, 1], precision=highest, preferred_element_type=jnp.float32)
    update1 = jnp.einsum("sqin,nr->sqir", panels[1], solved1, precision=highest, preferred_element_type=jnp.float32)
    updated = sectioned - update1
    return jnp.where(block_ids >= 2, updated, jnp.where(block_ids == 1, solved1, sectioned))
```

```python
import jax
import jax.numpy as jnp
from jax import lax
from jax.sharding import PartitionSpec as P


def broadcast(value, axis, source):
    kept = jnp.where(lax.axis_index(axis) == source, value, 0).astype(value.dtype)
    return lax.psum(kept, axis)


def per_device(rhs, panels, inverses):
    highest = lax.Precision.HIGH
    row_index = lax.axis_index("row")
    row_count = lax.axis_size("row")
    slot_count = rhs.shape[0]
    block_ids = (jnp.arange(slot_count, dtype=jnp.int32) * row_count + row_index)[
        :, None, None, None
    ]

    def solve_block(current, panel_index):
        owner_value = jnp.dot(
            inverses[panel_index], current, precision=highest, preferred_element_type=jnp.float32
        )
        solved = broadcast(owner_value, "row", panel_index)
        return (solved, solved)

    def apply_panel(tiles, solved):
        return jnp.einsum(
            "sqin,nr->sqir",
            lax.all_gather(tiles, "col", axis=3, tiled=True),
            solved,
            precision=highest,
            preferred_element_type=jnp.float32,
        )

    solved0, spread0 = solve_block(rhs[0, 0], 0)
    sectioned = rhs - apply_panel(panels[0], solved0)
    sectioned = jnp.where(block_ids >= 1, sectioned, solved0)
    solved1, spread1 = solve_block(sectioned[0, 0], 1)
    updated = sectioned - apply_panel(panels[1], solved1)
    return jnp.where(block_ids >= 2, updated, jnp.where(block_ids == 1, solved1, sectioned))


def solution(mesh):
    placed = (P(None, "row", None, "col"), P(None, None, "row", None, "col"), P())
    return jax.shard_map(
        per_device,
        mesh=mesh,
        in_specs=placed,
        out_specs=P(None, "row", None, "col"),
        check_vma=False,
    )
```

```python
import functools
import random

import jax
import jax.numpy as jnp
from jax import lax
from jax.experimental import pallas as pl
from jax.experimental.pallas import tpu as pltpu
from jax.sharding import PartitionSpec as P

MESH = pl.DeviceIdType.MESH
TREES = 3
CHUNK = 32


def grid_of(n):
    return {16: (4, 2, 2), 64: (4, 4, 4)}.get(n, (n, 1, 1))


def neighbours(n):
    dims = grid_of(n)
    place = lambda z, y, x: (z * dims[1] + y) * dims[2] + x
    table = []
    for axis in range(3):
        for way in (1, -1):
            line = []
            for q in range(n):
                at = [q // (dims[1] * dims[2]), q // dims[2] % dims[1], q % dims[2]]
                at[axis] += way
                line.append(place(*at) if 0 <= at[axis] < dims[axis] else -1)
            table.append(line)
    return table


@functools.lru_cache(maxsize=None)
def spanning_trees(n, root):
    table = neighbours(n)
    edges = [(u, line[u]) for line in table for u in range(n) if line[u] >= 0]
    into = {v: [e for e in edges if e[1] == v] for v in range(n)}
    draw = random.Random(7)
    best = None
    for _ in range(400 if n <= 16 else 25):
        used = {e: 0 for e in edges}
        depth = [{root: 0} for _ in range(TREES)]
        parent = [{} for _ in range(TREES)]
        while any(len(d) < n for d in depth):
            t = min(range(TREES), key=lambda i: (len(depth[i]), draw.random()))
            options = [e for e in edges if e[0] in depth[t] and e[1] not in depth[t]]
            rank = lambda e: (
                used[e],
                depth[t][e[0]] > 0 and e[0] == root,
                depth[t][e[0]],
                sum(used[o] == 0 for o in into[e[1]]),
                draw.random(),
            )
            u, v = min(options, key=rank)
            used[u, v] += 1
            depth[t][v] = depth[t][u] + 1
            parent[t][v] = u
        score = (max(used.values()), sum(c > 1 for c in used.values()), max(max(d.values()) for d in depth))
        if best is None or score < best[0]:
            best = (score, depth, parent)
    _, depth, parent = best
    levels = [[depth[t][q] for q in range(n)] for t in range(TREES)]
    parents = [[parent[t].get(q, (q + 1) % n) for q in range(n)] for t in range(TREES)]
    children = []
    for t in range(TREES):
        lists = [[v for v in range(n) if v != root and parent[t][v] == q] for q in range(n)]
        most = max(len(c) for c in lists)
        children.append([[c[i] if i < len(c) else -1 for c in lists] for i in range(most)])
    return levels, parents, children


def lookup(me, values):
    out = jnp.int32(values[0])
    for q, value in enumerate(values):
        if q and value != values[0]:
            out = jnp.where(me == q, jnp.int32(value), out)
    return out


def spread_kernel(n, root, exchange, *refs):
    if exchange:
        source, panels, out, full, send_sem, recv_sem, own_sem, pan_send, pan_recv, pan_own = refs
    else:
        source, out, send_sem, recv_sem, own_sem = refs
    me = lax.axis_index("row")
    levels, parents, children = spanning_trees(n, root)
    rows = out.shape[0]
    total = rows // CHUNK
    counts = [len(range(t, total, TREES)) for t in range(TREES)]

    level = [lookup(me, v) for v in levels]
    parent = [lookup(me, v) for v in parents]
    child = [[lookup(me, v) for v in lists] for lists in children]
    near = [lookup(me, v) for v in neighbours(n)]

    barrier = pltpu.get_barrier_semaphore()
    for other in near:

        @pl.when(other >= 0)
        def _():
            pl.semaphore_signal(barrier, inc=1, device_id={"row": other}, device_id_type=MESH)

    if exchange:
        core = lax.axis_index("col")
        pl.semaphore_signal(barrier, inc=1, device_id={"col": 1 - core}, device_id_type=MESH)
    peers = [sum(line[q] >= 0 for line in neighbours(n)) for q in range(n)]
    pl.semaphore_wait(barrier, lookup(me, peers) + (1 if exchange else 0))

    @pl.when(me == root)
    def _():
        own = pltpu.make_async_copy(source, out, own_sem)
        own.start()
        own.wait()

    def copy_to(t, j, device, slot):
        part = pl.ds(pl.multiple_of((TREES * j + t) * CHUNK, CHUNK), CHUNK)
        return pltpu.make_async_remote_copy(
            src_ref=out.at[part],
            dst_ref=out.at[part],
            send_sem=send_sem.at[slot, j],
            recv_sem=recv_sem.at[t, j],
            device_id={"row": device},
            device_id_type=MESH,
        )

    slots = []
    for t in range(TREES):
        first = sum(len(c) for c in children[:t])
        slots.append([first + i for i in range(len(children[t]))])

    def panel_copies():
        width = panels.shape[-1]
        columns = pl.ds(pl.multiple_of(core * width, width), width)
        pairs = []
        for k in range(panels.shape[0]):
            target = full.at[k, :, :, columns]
            pairs.append(
                (
                    pltpu.make_async_remote_copy(
                        src_ref=panels.at[k],
                        dst_ref=target,
                        send_sem=pan_send.at[k],
                        recv_sem=pan_recv.at[k],
                        device_id={"col": 1 - core},
                        device_id_type=MESH,
                    ),
                    pltpu.make_async_copy(panels.at[k], target, pan_own.at[k]),
                )
            )
        return pairs

    if exchange:
        for away, home in panel_copies():
            away.start()
            home.start()

    def step(s, carry):
        for t in range(TREES):
            j = s - level[t]

            @pl.when((j >= 0) & (j < counts[t]))
            def _():
                @pl.when(me != root)
                def _():
                    copy_to(t, j, parent[t], slots[t][0]).wait_recv()

                for i, slot in enumerate(slots[t]):

                    @pl.when(child[t][i] >= 0)
                    def _():
                        copy_to(t, j, child[t][i], slot).start()

        return carry

    deepest = max(max(v) for v in levels)
    lax.fori_loop(0, max(counts) + deepest, step, 0)

    for t in range(TREES):

        def finish(j, carry):
            for i, slot in enumerate(slots[t]):

                @pl.when(child[t][i] >= 0)
                def _():
                    copy_to(t, j, child[t][i], slot).wait_send()

            return carry

        lax.fori_loop(0, counts[t], finish, 0)

    if exchange:
        for away, home in panel_copies():
            away.wait()
            home.wait()


def spread(value, n, root, panels=None):
    exchange = panels is not None
    _, _, children = spanning_trees(n, root)
    chunks = -(-(value.shape[0] // CHUNK) // TREES)
    kept = jax.ShapeDtypeStruct(value.shape, value.dtype)
    vmem, anywhere = pl.BlockSpec(memory_space=pltpu.VMEM), pl.BlockSpec(memory_space=pl.ANY)
    scratch = [
        pltpu.SemaphoreType.DMA((sum(len(c) for c in children), chunks)),
        pltpu.SemaphoreType.DMA((TREES, chunks)),
        pltpu.SemaphoreType.DMA,
    ]
    in_specs, out_specs, out_shape, operands = [anywhere], vmem, kept, [value]
    if exchange:
        blocks, slots, rows, width = panels.shape
        in_specs, out_specs, operands = [anywhere] * 2, [vmem, anywhere], [value, panels]
        out_shape = [kept, jax.ShapeDtypeStruct((blocks, slots, rows, 2 * width), panels.dtype)]
        scratch += [pltpu.SemaphoreType.DMA((blocks,))] * 3
    return pl.pallas_call(
        functools.partial(spread_kernel, n, root, exchange),
        out_shape=out_shape,
        in_specs=in_specs,
        out_specs=out_specs,
        scratch_shapes=scratch,
        compiler_params=pltpu.CompilerParams(
            collective_id=1 + root, has_side_effects=True, vmem_limit_bytes=16 * 2**20
        ),
    )(*operands)


def per_device(rhs, panels, inverses):
    n = lax.axis_size("row")
    me = lax.axis_index("row")
    dot = functools.partial(
        jnp.dot, precision=lax.Precision.HIGH, preferred_element_type=jnp.float32
    )
    slots, _, rows, width = rhs.shape
    ids = (jnp.arange(slots, dtype=jnp.int32) * n + me)[:, None, None]
    own = rhs[:, 0]

    first, full = spread(own[0], n, 0, panels[:, :, 0])
    solved0 = dot(inverses[0], first)
    tall = full.reshape(2, slots * rows, full.shape[-1])
    sectioned = own - dot(tall[0], solved0).reshape(slots, rows, width)
    sectioned = jnp.where(ids >= 1, sectioned, solved0)
    solved1 = spread(dot(inverses[1], sectioned[0]), n, 1)
    updated = sectioned - dot(tall[1], solved1).reshape(slots, rows, width)
    result = jnp.where(ids >= 2, updated, jnp.where(ids == 1, solved1, sectioned))
    return result[:, None]


def solution(mesh):
    placed = (P(None, "row", None, "col"), P(None, None, "row", None, "col"), P())
    return jax.shard_map(
        per_device,
        mesh=mesh,
        in_specs=placed,
        out_specs=P(None, "row", None, "col"),
        check_vma=False,
    )
```

```python
import functools
import random

import jax
import jax.numpy as jnp
from jax import lax
from jax.experimental import pallas as pl
from jax.experimental.pallas import tpu as pltpu
from jax.sharding import PartitionSpec as P

MESH = pl.DeviceIdType.MESH
TREES = 3
CHUNK = 32
SLACK = 4


def grid_of(n):
    return {16: (4, 2, 2), 64: (4, 4, 4)}.get(n, (n, 1, 1))


def neighbours(n):
    dims = grid_of(n)
    place = lambda z, y, x: (z * dims[1] + y) * dims[2] + x
    table = []
    for axis in range(3):
        for way in (1, -1):
            line = []
            for q in range(n):
                at = [q // (dims[1] * dims[2]), q // dims[2] % dims[1], q % dims[2]]
                at[axis] += way
                line.append(place(*at) if 0 <= at[axis] < dims[axis] else -1)
            table.append(line)
    return table


@functools.lru_cache(maxsize=None)
def spanning_trees(n, root):
    table = neighbours(n)
    edges = [(u, line[u]) for line in table for u in range(n) if line[u] >= 0]
    into = {v: [e for e in edges if e[1] == v] for v in range(n)}
    draw = random.Random(7)
    best = None
    for _ in range(400 if n <= 16 else 25):
        used = {e: 0 for e in edges}
        depth = [{root: 0} for _ in range(TREES)]
        parent = [{} for _ in range(TREES)]
        while any(len(d) < n for d in depth):
            t = min(range(TREES), key=lambda i: (len(depth[i]), draw.random()))
            options = [e for e in edges if e[0] in depth[t] and e[1] not in depth[t]]
            rank = lambda e: (
                used[e],
                depth[t][e[0]] > 0 and e[0] == root,
                depth[t][e[0]],
                sum(used[o] == 0 for o in into[e[1]]),
                draw.random(),
            )
            u, v = min(options, key=rank)
            used[u, v] += 1
            depth[t][v] = depth[t][u] + 1
            parent[t][v] = u
        score = (max(used.values()), sum(c > 1 for c in used.values()), max(max(d.values()) for d in depth))
        if best is None or score < best[0]:
            best = (score, depth, parent)
    _, depth, parent = best
    levels = [[depth[t][q] for q in range(n)] for t in range(TREES)]
    parents = [[parent[t].get(q, (q + 1) % n) for q in range(n)] for t in range(TREES)]
    children = []
    for t in range(TREES):
        lists = [[v for v in range(n) if v != root and parent[t][v] == q] for q in range(n)]
        most = max(len(c) for c in lists)
        children.append([[c[i] if i < len(c) else -1 for c in lists] for i in range(most)])
    return levels, parents, children


def lookup(me, values):
    out = jnp.int32(values[0])
    for q, value in enumerate(values):
        if q and value != values[0]:
            out = jnp.where(me == q, jnp.int32(value), out)
    return out


def spread_kernel(n, root, exchange, *refs):
    if exchange:
        source, panels, out, full, send_sem, recv_sem, own_sem, pan_send, pan_recv, pan_own = refs
    else:
        source, out, send_sem, recv_sem, own_sem = refs
    me = lax.axis_index("row")
    levels, parents, children = spanning_trees(n, root)
    rows = out.shape[0]
    total = rows // CHUNK
    counts = [len(range(t, total, TREES)) for t in range(TREES)]

    level = [lookup(me, v) for v in levels]
    parent = [lookup(me, v) for v in parents]
    child = [[lookup(me, v) for v in lists] for lists in children]
    near = [lookup(me, v) for v in neighbours(n)]

    barrier = pltpu.get_barrier_semaphore()
    for other in near:

        @pl.when(other >= 0)
        def _():
            pl.semaphore_signal(barrier, inc=1, device_id={"row": other}, device_id_type=MESH)

    if exchange:
        core = lax.axis_index("col")
        pl.semaphore_signal(barrier, inc=1, device_id={"col": 1 - core}, device_id_type=MESH)
    peers = [sum(line[q] >= 0 for line in neighbours(n)) for q in range(n)]
    pl.semaphore_wait(barrier, lookup(me, peers) + (1 if exchange else 0))

    @pl.when(me == root)
    def _():
        own = pltpu.make_async_copy(source, out, own_sem)
        own.start()
        own.wait()

    def copy_to(t, j, device, slot):
        part = pl.ds(pl.multiple_of((TREES * j + t) * CHUNK, CHUNK), CHUNK)
        return pltpu.make_async_remote_copy(
            src_ref=out.at[part],
            dst_ref=out.at[part],
            send_sem=send_sem.at[slot, j],
            recv_sem=recv_sem.at[t, j],
            device_id={"row": device},
            device_id_type=MESH,
        )

    slots = []
    for t in range(TREES):
        first = sum(len(c) for c in children[:t])
        slots.append([first + i for i in range(len(children[t]))])

    def panel_copies():
        width = panels.shape[-1]
        columns = pl.ds(pl.multiple_of(core * width, width), width)
        pairs = []
        for k in range(panels.shape[0]):
            target = full.at[k, :, :, columns]
            pairs.append(
                (
                    pltpu.make_async_remote_copy(
                        src_ref=panels.at[k],
                        dst_ref=target,
                        send_sem=pan_send.at[k],
                        recv_sem=pan_recv.at[k],
                        device_id={"col": 1 - core},
                        device_id_type=MESH,
                    ),
                    pltpu.make_async_copy(panels.at[k], target, pan_own.at[k]),
                )
            )
        return pairs

    if exchange:
        for away, home in panel_copies():
            away.start()
            home.start()

    def step(s, carry):
        for t in range(TREES):
            j = s - SLACK * level[t]

            @pl.when((j >= 0) & (j < counts[t]))
            def _():
                @pl.when(me != root)
                def _():
                    copy_to(t, j, parent[t], slots[t][0]).wait_recv()

                for i, slot in enumerate(slots[t]):

                    @pl.when(child[t][i] >= 0)
                    def _():
                        copy_to(t, j, child[t][i], slot).start()

        return carry

    deepest = max(max(v) for v in levels)
    lax.fori_loop(0, max(counts) + SLACK * deepest, step, 0)

    for t in range(TREES):

        def finish(j, carry):
            for i, slot in enumerate(slots[t]):

                @pl.when(child[t][i] >= 0)
                def _():
                    copy_to(t, j, child[t][i], slot).wait_send()

            return carry

        lax.fori_loop(0, counts[t], finish, 0)

    if exchange:
        for away, home in panel_copies():
            away.wait()
            home.wait()


def spread(value, n, root, panels=None):
    exchange = panels is not None
    _, _, children = spanning_trees(n, root)
    chunks = -(-(value.shape[0] // CHUNK) // TREES)
    kept = jax.ShapeDtypeStruct(value.shape, value.dtype)
    vmem, anywhere = pl.BlockSpec(memory_space=pltpu.VMEM), pl.BlockSpec(memory_space=pl.ANY)
    scratch = [
        pltpu.SemaphoreType.DMA((sum(len(c) for c in children), chunks)),
        pltpu.SemaphoreType.DMA((TREES, chunks)),
        pltpu.SemaphoreType.DMA,
    ]
    in_specs, out_specs, out_shape, operands = [anywhere], vmem, kept, [value]
    if exchange:
        blocks, slots, rows, width = panels.shape
        in_specs, out_specs, operands = [anywhere] * 2, [vmem, anywhere], [value, panels]
        out_shape = [kept, jax.ShapeDtypeStruct((blocks, slots, rows, 2 * width), panels.dtype)]
        scratch += [pltpu.SemaphoreType.DMA((blocks,))] * 3
    return pl.pallas_call(
        functools.partial(spread_kernel, n, root, exchange),
        out_shape=out_shape,
        in_specs=in_specs,
        out_specs=out_specs,
        scratch_shapes=scratch,
        compiler_params=pltpu.CompilerParams(
            collective_id=1 + root, has_side_effects=True, vmem_limit_bytes=16 * 2**20
        ),
    )(*operands)


def per_device(rhs, panels, inverses):
    n = lax.axis_size("row")
    me = lax.axis_index("row")
    dot = functools.partial(
        jnp.dot, precision=lax.Precision.HIGH, preferred_element_type=jnp.float32
    )
    slots, _, rows, width = rhs.shape
    ids = (jnp.arange(slots, dtype=jnp.int32) * n + me)[:, None, None]
    own = rhs[:, 0]

    first, full = spread(own[0], n, 0, panels[:, :, 0])
    solved0 = dot(inverses[0], first)
    tall = full.reshape(2, slots * rows, full.shape[-1])
    sectioned = own - dot(tall[0], solved0).reshape(slots, rows, width)
    sectioned = jnp.where(ids >= 1, sectioned, solved0)
    solved1 = spread(dot(inverses[1], sectioned[0]), n, 1)
    updated = sectioned - dot(tall[1], solved1).reshape(slots, rows, width)
    result = jnp.where(ids >= 2, updated, jnp.where(ids == 1, solved1, sectioned))
    return result[:, None]


def solution(mesh):
    placed = (P(None, "row", None, "col"), P(None, None, "row", None, "col"), P())
    return jax.shard_map(
        per_device,
        mesh=mesh,
        in_specs=placed,
        out_specs=P(None, "row", None, "col"),
        check_vma=False,
    )
```
